256 devices in a mesh: ctx: 32 (over y, z), head: 8 (over x, core).
Axes of the slice: x: 4, y: 4, z: 8, core: 2. Of those that a mesh axis runs over, the one named last changes fastest.
Arguments:
- exponential_probe_vectors: bfloat16 [16384, 4096], P('ctx', 'head'), may hold values from -10 to 10
- exponential_lookup_vectors: bfloat16 [16384, 1024], P('ctx', 'head'), may hold values from -10 to 10
- exponential_content_vectors: bfloat16 [16384, 1024], P('ctx', 'head'), may hold values from -4 to 4
- linear_mixer_probe_vectors: bfloat16 [16384, 4096], P('ctx', 'head'), may hold values from -512 to 512
- linear_mixer_lookup_vectors: bfloat16 [16384, 4096], P('ctx', 'head'), may hold values from -4 to 4
- fading_powers: int32 [32], P('head'), may hold values from 5 to 19
- shrink_positions: int32 [16384], P('ctx'), may hold values 0 or 1
- final_rescale_weights: bfloat16 [4096], P('head'), may hold values from 0.099609375 to 1.8984375
Outputs:
- lightning_out: bfloat16 [16384, 4096], P('ctx', 'head')
The draws below stay inside these ranges and needn't reach their ends.
All inputs are finite; a program needn't handle non-finite values. No bound on the sum of `shrink_positions` on one device may be relied on, other than what follows from the above.
Results may differ from the reference program's by a relative error of at most 0.023.
Values may be sent and summed in bfloat16 or wider, within the bound.
A program may use at most 64 MiB of HBM per device.

```python
import math
import jax
import jax.numpy as jnp
from jax import lax

HQ = 32
HK = 8
HD = 128
SPAN = 256
TOKEN_TOTAL = 16384


def draw_exponential_probe_vectors(key, part):
    key = jax.random.fold_in(key, 1)
    entries = 1.5 * jax.random.truncated_normal(key, -4.0, 4.0, (TOKEN_TOTAL, HQ, HD), jnp.float32)
    return entries.reshape(TOKEN_TOTAL, HQ * HD).astype(jnp.bfloat16)


def draw_exponential_lookup_vectors(key, part):
    key = jax.random.fold_in(key, 2)
    entries = jax.random.truncated_normal(key, -4.0, 4.0, (TOKEN_TOTAL, HK, HD), jnp.float32)
    return entries.reshape(TOKEN_TOTAL, HK * HD).astype(jnp.bfloat16)


def draw_linear_mixer_probe_vectors(key, part):
    key = jax.random.fold_in(key, 3)
    head_scale = jnp.power(10.0, jnp.arange(HQ, dtype=jnp.float32) / (HQ - 1))
    row_scale = jnp.exp(jax.random.uniform(jax.random.fold_in(key, 1), (TOKEN_TOTAL,), jnp.float32, 0.0, math.log(10.0)))
    entries = jax.random.truncated_normal(jax.random.fold_in(key, 2), -4.0, 4.0, (TOKEN_TOTAL, HQ, HD), jnp.float32)
    scaled = entries * row_scale[:, None, None] * head_scale[None, :, None]
    return scaled.reshape(TOKEN_TOTAL, HQ * HD).astype(jnp.bfloat16)


def set_ends(values, own_key, least, largest):
    index_at = [jax.random.randint(jax.random.fold_in(own_key, axis), (), 0, length) for axis, length in enumerate(values.shape)]
    main_axis = values.shape.index(max(values.shape))
    beside = index_at[:main_axis] + [(index_at[main_axis] + 1) % values.shape[main_axis]] + index_at[main_axis + 1:]
    return values.at[tuple(index_at)].set(least).at[tuple(beside)].set(largest)


def block_levels(rng, extent, cuts, least, high):
    loudness = 1.0
    for dim, parts in cuts:
        draws = jax.random.uniform(jax.random.fold_in(jax.random.fold_in(rng, 6), dim), (parts,), jnp.float32, least / len(cuts), high / len(cuts))
        loudness = loudness * jnp.repeat(jnp.exp(draws), extent[dim] // parts).reshape((-1,) + (1,) * (len(extent) - 1 - dim))
    return loudness


def bell_draw(own_key, dims, spread, most, pieces=(), kind=jnp.bfloat16):
    values = jax.random.normal(own_key, dims, jnp.float32) * spread
    if len(pieces) > 0:
        values = block_levels(own_key, dims, pieces, -0.22, 0.18) * values
    return jnp.clip(values, min=-most, max=most).astype(kind)


def setup_inputs(seed: int = 0) -> dict:
    key_of = jax.random.split(jax.random.key(seed), 9)
    exponential_probe_vectors = draw_exponential_probe_vectors(jax.random.fold_in(key_of[8], 71), 0)
    exponential_lookup_vectors = draw_exponential_lookup_vectors(jax.random.fold_in(key_of[8], 71), 0)
    exponential_content_vectors = bell_draw(key_of[2], (TOKEN_TOTAL, HK * HD), 1.0, 4.0, ((0, 32), (1, 8)))
    linear_mixer_probe_vectors = draw_linear_mixer_probe_vectors(jax.random.fold_in(key_of[8], 71), 0)
    linear_mixer_lookup_vectors = bell_draw(key_of[4], (TOKEN_TOTAL, HQ * HD), 1.0, 4.0, ((0, 32), (1, 8)))
    fading_powers = set_ends(jax.random.randint(key_of[5], (HQ,), 5, 20), jax.random.fold_in(key_of[5], 1), 5, 19).astype(jnp.int32)
    shrink_positions = set_ends((jax.random.randint(key_of[6], (TOKEN_TOTAL,), 0, 2048) < 1).astype(jnp.int32), jax.random.fold_in(key_of[6], 1), 0, 1)
    final_rescale_weights = jnp.clip(1.0 + 0.18 * jax.random.normal(key_of[7], (HQ * HD,), jnp.float32), 0.099609375, 1.8984375).astype(jnp.bfloat16)
    return dict(exponential_probe_vectors=exponential_probe_vectors, exponential_lookup_vectors=exponential_lookup_vectors, exponential_content_vectors=exponential_content_vectors, linear_mixer_probe_vectors=linear_mixer_probe_vectors, linear_mixer_lookup_vectors=linear_mixer_lookup_vectors, fading_powers=fading_powers, shrink_positions=shrink_positions, final_rescale_weights=final_rescale_weights)


norm_epsilon = 1e-06

def sequence_position(row_index):
    device_block = row_index // (2 * SPAN)
    offset_in = row_index % (2 * SPAN)
    block_count = TOKEN_TOTAL // SPAN
    return jnp.where(offset_in < SPAN, device_block * SPAN + offset_in, (block_count - 1 - device_block) * SPAN + offset_in - SPAN).astype(jnp.int32)

def storage_row(position):
    block_id = position // SPAN
    within = position % SPAN
    block_count = TOKEN_TOTAL // SPAN
    first_half = block_id < block_count // 2
    device_block = jnp.where(first_half, block_id, block_count - 1 - block_id)
    offset_in = jnp.where(first_half, within, within + SPAN)
    return (device_block * 2 * SPAN + offset_in).astype(jnp.int32)

def softmax_layer(exponential_probe_vectors, exponential_lookup_vectors, exponential_content_vectors, stacking_sequence_plan, positions):
    group_size = HQ // HK
    query_seq = exponential_probe_vectors[stacking_sequence_plan].reshape(TOKEN_TOTAL, HK, group_size, HD).transpose(1, 0, 2, 3)
    key_seq = exponential_lookup_vectors[stacking_sequence_plan].reshape(TOKEN_TOTAL, HK, HD).transpose(1, 0, 2)
    value_seq = exponential_content_vectors[stacking_sequence_plan].reshape(TOKEN_TOTAL, HK, HD).transpose(1, 0, 2)
    scaling = 1.0 / math.sqrt(HD)
    block_rows = math.gcd(512, TOKEN_TOTAL)
    starts = jnp.arange(TOKEN_TOTAL // block_rows, dtype=jnp.int32) * block_rows

    def one_group(operands):
        query_group, key_group, value_group = operands
        key_float = key_group.astype(jnp.float32)
        value_float = value_group.astype(jnp.float32)

        def one_block(start):
            query_block = lax.dynamic_slice_in_dim(query_group, start, block_rows, 0).astype(jnp.float32)
            query_pos = start + jnp.arange(block_rows, dtype=jnp.int32)
            scores = jnp.einsum('bgd,sd->bgs', query_block, key_float) * scaling
            visible = positions[None, None, :] <= query_pos[:, None, None]
            highest = lax.optimization_barrier(jnp.max(jnp.where(visible, scores, -jnp.inf), axis=2, keepdims=True))
            weights = jnp.where(visible, jnp.exp(scores - highest), 0.0)
            totals = lax.optimization_barrier(jnp.sum(weights, axis=2))
            rounded = lax.optimization_barrier(weights.astype(jnp.bfloat16)).astype(jnp.float32)
            summed = jnp.einsum('bgs,sd->bgd', rounded, value_float)
            return summed / totals[:, :, None]
        return lax.map(one_block, starts)
    outputs = lax.map(one_group, (query_seq, key_seq, value_seq))
    outputs = outputs.reshape(HK, TOKEN_TOTAL, group_size, HD).transpose(1, 0, 2, 3)
    return outputs.reshape(TOKEN_TOTAL, HQ * HD).astype(jnp.bfloat16)

def linear_recurrent_mixer(exponential_weighted_mixer, linear_mixer_probe_vectors, linear_mixer_lookup_vectors, fading_powers, shrink_positions, stacking_sequence_plan):
    block_count = TOKEN_TOTAL // SPAN
    query_blocks = linear_mixer_probe_vectors[stacking_sequence_plan].astype(jnp.float32).reshape(block_count, SPAN, HQ, HD)
    key_blocks = linear_mixer_lookup_vectors[stacking_sequence_plan].astype(jnp.float32).reshape(block_count, SPAN, HQ, HD)
    value_blocks = exponential_weighted_mixer.astype(jnp.float32).reshape(block_count, SPAN, HQ, HD)
    fading_speeds = jnp.exp2(-fading_powers.astype(jnp.float32))
    stride_natural_log = -fading_speeds[None, :] - 0.5 * shrink_positions[stacking_sequence_plan].astype(jnp.float32)[:, None]
    step_blocks = stride_natural_log.reshape(block_count, SPAN, HQ)
    lower = (jnp.arange(SPAN)[:, None] >= jnp.arange(SPAN)[None, :])[None]

    def block_step(state, operands):
        query_b, key_b, value_b, step_b = operands
        running = jnp.cumsum(step_b, axis=0)
        final_log = running[-1]
        scores = jnp.einsum('thd,shd->hts', query_b, key_b)
        distance = running.T[:, :, None] - running.T[:, None, :]
        decayed = jnp.where(lower, scores * jnp.exp(jnp.where(lower, distance, 0.0)), 0.0)
        rounded = lax.optimization_barrier(decayed.astype(jnp.bfloat16)).astype(jnp.float32)
        intra = jnp.einsum('hts,shd->thd', rounded, value_b)
        inter = jnp.einsum('thd,hde->the', query_b * jnp.exp(running)[:, :, None], state, precision=lax.Precision.HIGHEST)
        update = jnp.einsum('thd,the->hde', key_b * jnp.exp(final_log[None, :] - running)[:, :, None], value_b, precision=lax.Precision.HIGHEST)
        new_state = jnp.exp(final_log)[:, None, None] * state + update
        return (new_state, intra + inter)
    final_state, combined_result = lax.scan(block_step, jnp.zeros((HQ, HD, HD), jnp.float32), (query_blocks, key_blocks, value_blocks, step_blocks))
    return combined_result.reshape(TOKEN_TOTAL, HQ * HD)

def reference(exponential_probe_vectors, exponential_lookup_vectors, exponential_content_vectors, linear_mixer_probe_vectors, linear_mixer_lookup_vectors, fading_powers, shrink_positions, final_rescale_weights):
    positions = jnp.arange(TOKEN_TOTAL, dtype=jnp.int32)
    stacking_sequence_plan = storage_row(positions)
    exponential_weighted_mixer = softmax_layer(exponential_probe_vectors, exponential_lookup_vectors, exponential_content_vectors, stacking_sequence_plan, positions)
    combined_result = linear_recurrent_mixer(exponential_weighted_mixer, linear_mixer_probe_vectors, linear_mixer_lookup_vectors, fading_powers, shrink_positions, stacking_sequence_plan)
    mean_square = lax.optimization_barrier(jnp.mean(combined_result * combined_result, axis=1))
    normed = combined_result * lax.rsqrt(mean_square + norm_epsilon)[:, None] * final_rescale_weights.astype(jnp.float32)[None, :]
    back = sequence_position(positions)
    return normed[back].astype(jnp.bfloat16)
```

```python
import functools
import math

import jax
import jax.numpy as jnp
from jax import lax
from jax.experimental import pallas as pl
from jax.experimental.pallas import tpu as pltpu
from jax.sharding import PartitionSpec as P

HQ = 32
HD = 128
SPAN = 256
HEADS = 4
ROWS_Y = 4
RING = 8
CTX = 32
GROUP = 8
NORM_EPSILON = 1e-06
LOW = -1e30
MESH = pl.DeviceIdType.MESH
F32 = jnp.float32
BF16 = jnp.bfloat16
NT = (((1,), (1,)), ((), ()))
NN = (((1,), (0,)), ((), ()))
TN = (((0,), (0,)), ((), ()))


def dot(a, b, dims=NN):
    return lax.dot_general(a, b, dims, preferred_element_type=F32)


def eye_mask():
    return lax.broadcasted_iota(jnp.int32, (128, 128), 0) == lax.broadcasted_iota(
        jnp.int32, (128, 128), 1
    )


def column_to_row(column):
    return jnp.sum(jnp.where(eye_mask(), column, 0.0), axis=0, keepdims=True)


def row_to_column(row):
    spread = jnp.where(eye_mask(), jnp.broadcast_to(row, (128, 128)), 0.0)
    return jnp.broadcast_to(jnp.sum(spread, axis=1, keepdims=True), (128, 128))


def twice(x):
    return jnp.concatenate([x, x], axis=1)


def split_queries(source, target):
    scale = math.log2(math.e) / math.sqrt(HD)
    for h in range(HEADS):
        scaled = source[:, h * HD : (h + 1) * HD].astype(F32) * scale
        high = scaled.astype(BF16)
        low = (scaled - high.astype(F32)).astype(BF16)
        target[h * SPAN : (h + 1) * SPAN, 0:HD] = high
        target[h * SPAN : (h + 1) * SPAN, HD : 2 * HD] = low


def attend(queries, keys, values, size, accum, highest, scores, masked=False):
    def product(h, slot):
        k = twice(keys[...].reshape(size, HD))
        s = dot(queries[h * SPAN : (h + 1) * SPAN, :], k, NT)
        if masked:
            row = lax.broadcasted_iota(jnp.int32, (SPAN, size), 0)
            col = lax.broadcasted_iota(jnp.int32, (SPAN, size), 1)
            s = jnp.where(col <= row, s, LOW)
        scores[slot, :, 0:size] = s

    def fold(h, slot):
        rows = slice(h * SPAN, (h + 1) * SPAN)
        s = scores[slot, :, 0:size]
        old = highest[rows, :]
        new = jnp.maximum(
            old, jnp.broadcast_to(jnp.max(s, axis=1, keepdims=True), (SPAN, HD))
        )
        factor = jnp.exp2(old - new)
        p = jnp.exp2(s - jnp.concatenate([new] * (size // HD), axis=1)).astype(BF16)
        v = values[...].reshape(size, HD)
        v = jnp.concatenate([v, jnp.ones_like(v)], axis=1)
        accum[rows, :] = accum[rows, :] * twice(factor) + dot(p, v)
        highest[rows, :] = new

    product(0, 0)
    for h in range(HEADS):
        if h + 1 < HEADS:
            product(h + 1, (h + 1) % 2)
        fold(h, h % 2)


def attention_kernel(
    q_ref, k_ref, v_ref, out_ref,
    qbuf, kbuf, vbuf, qs, accum, highest, scores, osend, lsend, orecv, lrecv,
    qsend_sem, qrecv_sem, kvsend_sem, kvrecv_sem, osend_sem, orecv_sem, lsend_sem, lrecv_sem,
):
    me = lax.axis_index("ctx")
    y, z = me // RING, lax.rem(me, RING)
    right = y * RING + lax.rem(z + 1, RING)
    left = y * RING + lax.rem(z + RING - 1, RING)

    def row_of(r):
        return lax.rem(y + r, ROWS_Y)

    def partner(r):
        return row_of(r) * RING + z

    barrier = pltpu.get_barrier_semaphore()
    for other in (left, right, partner(1), partner(2), partner(3)):
        pl.semaphore_signal(barrier, inc=1, device_id={"ctx": other}, device_id_type=MESH)
    pl.semaphore_wait(barrier, 5)

    def ring_copy(half, way, piece, s):
        buf, own = (kbuf, k_ref) if piece == 0 else (vbuf, v_ref)
        target = 1 if s == 3 else 2 * (s + 1) + way
        src = own.at[half] if s == 0 else buf.at[half, 2 * s + way]
        return pltpu.make_async_remote_copy(
            src_ref=src,
            dst_ref=buf.at[half, target],
            send_sem=kvsend_sem.at[half, way, piece, s],
            recv_sem=kvrecv_sem.at[half, way, piece, s],
            device_id={"ctx": right if way == 0 else left},
            device_id_type=MESH,
        )

    def pieces(way, s):
        return (0, 1) if s < 3 else (way,)

    def ring_send(half, s):
        for piece in (0, 1):
            for way in (0, 1):
                if piece in pieces(way, s):
                    ring_copy(half, way, piece, s).start()

    def ring_step(half, s):
        for piece in (0, 1):
            for way in (0, 1):
                if piece in pieces(way, s - 1):
                    ring_copy(half, way, piece, s - 1).wait_recv()
                if s < 4 and piece in pieces(way, s):
                    ring_copy(half, way, piece, s).start()

    def query_copy(r, half):
        return pltpu.make_async_remote_copy(
            src_ref=q_ref.at[half],
            dst_ref=qbuf.at[ROWS_Y - r, half],
            send_sem=qsend_sem.at[r, half],
            recv_sem=qrecv_sem.at[ROWS_Y - r, half],
            device_id={"ctx": partner(r)},
            device_id_type=MESH,
        )

    def query_arrival(r, half):
        return pltpu.make_async_remote_copy(
            src_ref=q_ref.at[half],
            dst_ref=qbuf.at[r, half],
            send_sem=qsend_sem.at[r, half],
            recv_sem=qrecv_sem.at[r, half],
            device_id={"ctx": partner(r)},
            device_id_type=MESH,
        )

    def result_copies(r, half, back):
        slot = r if back else ROWS_Y - r
        return (
            pltpu.make_async_remote_copy(
                src_ref=osend.at[r, half],
                dst_ref=orecv.at[slot, half],
                send_sem=osend_sem.at[r, half],
                recv_sem=orecv_sem.at[slot, half],
                device_id={"ctx": partner(r)},
                device_id_type=MESH,
            ),
            pltpu.make_async_remote_copy(
                src_ref=lsend.at[r, half],
                dst_ref=lrecv.at[slot, half],
                send_sem=lsend_sem.at[r, half],
                recv_sem=lrecv_sem.at[slot, half],
                device_id={"ctx": partner(r)},
                device_id_type=MESH,
            ),
        )

    ring_send(0, 0)
    for r in (3, 1, 2):

        @pl.when(y > row_of(r))
        def _(r=r):
            query_copy(r, 0).start()

        query_copy(r, 1).start()

    def clear(a):
        accum[a] = jnp.zeros((HEADS * SPAN, 2 * HD), F32)
        highest[a] = jnp.full((HEADS * SPAN, HD), LOW, F32)

    def single(half, slot, masked=False):
        attend(
            qs.at[half], kbuf.at[half, slot], vbuf.at[half, slot], SPAN,
            accum.at[half], highest.at[half], scores, masked,
        )

    kbuf[0, 0] = k_ref[0]
    vbuf[0, 0] = v_ref[0]
    kbuf[1, 0] = k_ref[1]
    vbuf[1, 0] = v_ref[1]
    for half in (0, 1):
        split_queries(q_ref.at[half], qs.at[half])
        clear(half)
        single(half, 0, masked=True)

    def pair(s):
        attend(
            qs.at[1], kbuf.at[0, 2 * s : 2 * s + 2], vbuf.at[0, 2 * s : 2 * s + 2], 2 * SPAN,
            accum.at[1], highest.at[1], scores,
        )

    for s in (1, 2, 3):
        ring_step(0, s)
        if s == 2:
            ring_send(1, 0)
        pair(s)

        @pl.loop(0, 2)
        def _(way, s=s):
            @pl.when(lax.rem(z + RING - s + 2 * s * way, RING) < z)
            def _():
                single(0, 2 * s + way)

    ring_step(0, 4)
    pair(0)

    @pl.when(z >= 4)
    def _():
        single(0, 1)

    def stream(slot, half, a):
        @pl.loop(0, 2)
        def _(c):
            attend(
                qs.at[slot], kbuf.at[half, pl.ds(4 * c, 4)], vbuf.at[half, pl.ds(4 * c, 4)],
                4 * SPAN, accum.at[a], highest.at[a], scores,
            )

    def emit(r, half, a):
        for h in range(HEADS):
            rows = slice(h * SPAN, (h + 1) * SPAN)
            total = accum[a, rows, HD : 2 * HD]
            osend[r, half, :, h * HD : (h + 1) * HD] = (accum[a, rows, 0:HD] / total).astype(BF16)
            level = highest[a, rows, :] + jnp.log2(total)
            for g in range(2):
                lsend[r, half, 2 * h + g : 2 * h + g + 1, :] = column_to_row(
                    level[g * 128 : (g + 1) * 128, :]
                )
        for copy in result_copies(r, half, False):
            copy.start()

    for turn, r in enumerate((3, 1, 2)):
        above = row_of(r) > y

        @pl.when(above)
        def _(r=r):
            query_arrival(r, 0).wait_recv()

        query_arrival(r, 1).wait_recv()
        split_queries(qbuf.at[r, jnp.where(above, 0, 1)], qs.at[2])
        clear(1 + r)
        stream(2, 0, 1 + r)

        @pl.when(above)
        def _(r=r):
            emit(r, 0, 1 + r)

        ring_step(1, turn + 1)

    ring_step(1, 4)

    for r in (3, 1, 2):
        above = row_of(r) > y

        @pl.when(above)
        def _(r=r):
            clear(1 + r)

        split_queries(qbuf.at[r, 1], qs.at[2])
        stream(2, jnp.where(above, 0, 1), 1 + r)
        emit(r, 1, 1 + r)

    @pl.loop(1, RING)
    def _(slot):
        s = slot // 2
        away = jnp.where(slot == 1, 4, jnp.where(lax.rem(slot, 2) == 0, RING - s, s))

        @pl.when(lax.rem(z + away, RING) > z)
        def _():
            single(1, slot)

    def combine(half):
        for r in (1, 2, 3):
            if half == 1:
                for copy in result_copies(r, 1, True):
                    copy.wait_recv()
            else:
                below = row_of(r) < y

                @pl.when(below)
                def _(r=r):
                    for copy in result_copies(r, 0, True):
                        copy.wait_recv()

                @pl.when(jnp.logical_not(below))
                def _(r=r):
                    orecv[r, 0] = jnp.zeros((SPAN, HEADS * HD), BF16)
                    lrecv[r, 0] = jnp.full((8, 128), LOW, F32)

        for h in range(HEADS):
            for g in range(2):
                rows = slice(h * SPAN + g * 128, h * SPAN + (g + 1) * 128)
                part = slice(g * 128, (g + 1) * 128)
                cols = slice(h * HD, (h + 1) * HD)
                total = accum[half, rows, HD : 2 * HD]
                levels = [highest[half, rows, :] + jnp.log2(total)]
                values = [accum[half, rows, 0:HD] / total]
                for r in (1, 2, 3):
                    levels.append(row_to_column(lrecv[r, half, 2 * h + g : 2 * h + g + 1, :]))
                    values.append(orecv[r, half, part, cols].astype(F32))
                top = functools.reduce(jnp.maximum, levels)
                weights = [jnp.exp2(level - top) for level in levels]
                mixed = sum(w * v for w, v in zip(weights, values)) / sum(weights)
                out_ref[half, part, cols] = mixed.astype(BF16)

    combine(0)
    combine(1)

    for half in (0, 1):
        for s in range(4):
            for way in (0, 1):
                for piece in pieces(way, s):
                    ring_copy(half, way, piece, s).wait_send()
    for r in (1, 2, 3):

        @pl.when(y > row_of(r))
        def _(r=r):
            query_copy(r, 0).wait_send()

        query_copy(r, 1).wait_send()

        @pl.when(row_of(r) > y)
        def _(r=r):
            for copy in result_copies(r, 0, False):
                copy.wait_send()

        for copy in result_copies(r, 1, False):
            copy.wait_send()


def lightning_kernel(
    a_ref, q_ref, k_ref, shrink_ref, fading_ref, gain_ref, out_ref,
    usend, urecv, ssend, srecv, mixed, qd, sqsend, sqrecv,
    usend_sem, urecv_sem, ssend_sem, srecv_sem, sqsend_sem, sqrecv_sem,
):
    me = lax.axis_index("ctx")
    head = lax.axis_index("head")

    barrier = pltpu.get_barrier_semaphore()

    @pl.loop(1, CTX)
    def _(k):
        pl.semaphore_signal(
            barrier, inc=1, device_id={"ctx": lax.rem(me + k, CTX)}, device_id_type=MESH
        )

    @pl.loop(1, GROUP)
    def _(k):
        pl.semaphore_signal(
            barrier, inc=1, device_id={"head": lax.rem(head + k, GROUP)}, device_id_type=MESH
        )

    row = lax.broadcasted_iota(jnp.int32, (SPAN, SPAN), 0)
    col = lax.broadcasted_iota(jnp.int32, (SPAN, SPAN), 1)
    lower = col <= row
    step_col = (lax.broadcasted_iota(jnp.int32, (SPAN, HD), 0) + 1).astype(F32)
    step_row = (lax.broadcasted_iota(jnp.int32, (8, SPAN), 1) + 1).astype(F32)
    for c in (0, 1):
        shrink = shrink_ref[c : c + 1, :].astype(F32)
        counts_col = jnp.broadcast_to(
            jnp.sum(jnp.where(lower, jnp.broadcast_to(shrink, (SPAN, SPAN)), 0.0), axis=1, keepdims=True),
            (SPAN, HD),
        )
        counts_row = dot(
            jnp.broadcast_to(shrink, (8, SPAN)).astype(BF16),
            jnp.where(row <= col, 1.0, 0.0).astype(BF16),
        )
        count = jnp.broadcast_to(jnp.sum(shrink, axis=1, keepdims=True), (16, HD))
        for h in range(HEADS):
            cols = slice(h * HD, (h + 1) * HD)
            power = fading_ref[h].astype(F32)
            speed_col = jnp.exp2(jnp.full((SPAN, HD), -power, F32))
            speed_row = jnp.exp2(jnp.full((8, SPAN), -power, F32))
            run_col = -speed_col * step_col - 0.5 * counts_col
            run_row = -speed_row * step_row - 0.5 * counts_row
            last = run_col[SPAN - 1 : SPAN, :]
            q = q_ref[c, :, cols]
            k = k_ref[c, :, cols]
            a = a_ref[c, :, cols]
            gap = jnp.minimum(twice(run_col) - jnp.broadcast_to(run_row[0:1, :], (SPAN, SPAN)), 0.0)
            decayed = jnp.where(lower, dot(q, k, NT) * jnp.exp(gap), 0.0).astype(BF16)
            mixed[c, :, cols] = dot(decayed, a)
            qd[c, :, cols] = (q.astype(F32) * jnp.exp(run_col)).astype(BF16)
            kd = (k.astype(F32) * jnp.exp(last - run_col)).astype(BF16)
            update = dot(kd, a, TN).astype(BF16)
            for part in range(8):
                usend[c, 8 * h + part, 0:16, :] = update[16 * part : 16 * (part + 1), :]
                usend[c, 8 * h + part, 16:32, :] = count.astype(BF16)

    pl.semaphore_wait(barrier, CTX - 1 + GROUP - 1)

    def update_copy(k):
        other = lax.rem(me + k, CTX)
        return pltpu.make_async_remote_copy(
            src_ref=usend.at[:, other],
            dst_ref=urecv.at[:, me],
            send_sem=usend_sem,
            recv_sem=urecv_sem,
            device_id={"ctx": other},
            device_id_type=MESH,
        )

    def update_all():
        return pltpu.make_async_remote_copy(
            src_ref=usend.at[:, 0 : CTX - 1],
            dst_ref=urecv.at[:, 0 : CTX - 1],
            send_sem=usend_sem,
            recv_sem=urecv_sem,
            device_id={"ctx": lax.rem(me + 1, CTX)},
            device_id_type=MESH,
        )

    def state_copy(k):
        other = lax.rem(me + k, CTX)
        return pltpu.make_async_remote_copy(
            src_ref=ssend.at[:, other],
            dst_ref=srecv.at[:, me],
            send_sem=ssend_sem,
            recv_sem=srecv_sem,
            device_id={"ctx": other},
            device_id_type=MESH,
        )

    def state_all():
        return pltpu.make_async_remote_copy(
            src_ref=ssend.at[:, 0 : CTX - 1],
            dst_ref=srecv.at[:, 0 : CTX - 1],
            send_sem=ssend_sem,
            recv_sem=srecv_sem,
            device_id={"ctx": lax.rem(me + 1, CTX)},
            device_id_type=MESH,
        )

    @pl.loop(1, CTX)
    def _(k):
        update_copy(k).start()

    for c in (0, 1):
        urecv[c, me] = usend[c, me]
    update_all().wait_recv()

    block_step = SPAN * jnp.exp2(jnp.full((16, HD), -fading_ref[me // 8].astype(F32), F32))
    state = jnp.zeros((16, HD), F32)
    for c, b in [(0, b) for b in range(CTX)] + [(1, b) for b in reversed(range(CTX))]:
        ssend[c, b] = state.astype(BF16)
        message = urecv[c, b].astype(F32)
        state = jnp.exp(-block_step - 0.5 * message[16:32, :]) * state + message[0:16, :]

    @pl.loop(1, CTX)
    def _(k):
        state_copy(k).start()

    for c in (0, 1):
        srecv[c, me] = ssend[c, me]
    state_all().wait_recv()

    for c in (0, 1):
        squares = jnp.zeros((SPAN, HD), F32)
        for h in range(HEADS):
            cols = slice(h * HD, (h + 1) * HD)
            state_h = srecv[c, 8 * h : 8 * h + 8].reshape(HD, HD)
            value = mixed[c, :, cols] + dot(qd[c, :, cols], state_h)
            mixed[c, :, cols] = value
            squares = squares + value * value
        column = jnp.broadcast_to(jnp.sum(squares, axis=1, keepdims=True), (SPAN, HD))
        for g in range(2):
            sqsend[2 * c + g : 2 * c + g + 1, :] = column_to_row(column[g * 128 : (g + 1) * 128, :])
    sqsend[4:8, :] = jnp.zeros((4, 128), F32)

    def square_copy(k):
        other = lax.rem(head + k, GROUP)
        return pltpu.make_async_remote_copy(
            src_ref=sqsend,
            dst_ref=sqrecv.at[GROUP - k],
            send_sem=sqsend_sem.at[k],
            recv_sem=sqrecv_sem.at[GROUP - k],
            device_id={"head": other},
            device_id_type=MESH,
        )

    for k in range(1, GROUP):
        square_copy(k).start()
    total = sqsend[...]
    for k in range(1, GROUP):
        square_copy(k).wait_recv()
        total = total + sqrecv[GROUP - k]
    scale = lax.rsqrt(total * (1.0 / (HQ * HD)) + NORM_EPSILON)
    for c in (0, 1):
        for g in range(2):
            column = row_to_column(scale[2 * c + g : 2 * c + g + 1, :])
            part = slice(g * 128, (g + 1) * 128)
            for h in range(HEADS):
                cols = slice(h * HD, (h + 1) * HD)
                gain = jnp.broadcast_to(gain_ref[0:1, cols].astype(F32), (128, HD))
                out_ref[c, part, cols] = (mixed[c, part, cols] * column * gain).astype(BF16)

    update_all().wait_send()
    state_all().wait_send()
    for k in range(1, GROUP):
        square_copy(k).wait_send()


VMEM = pl.BlockSpec(memory_space=pltpu.VMEM)
SMEM = pl.BlockSpec(memory_space=pltpu.SMEM)
WIDE = HEADS * HD


def per_device(q, k, v, lq, lk, fading, shrink, gain):
    dma = pltpu.SemaphoreType.DMA
    attention = pl.pallas_call(
        attention_kernel,
        out_shape=jax.ShapeDtypeStruct((2, SPAN, WIDE), BF16),
        in_specs=[VMEM] * 3,
        out_specs=VMEM,
        scratch_shapes=[
            pltpu.VMEM((ROWS_Y, 2, SPAN, WIDE), BF16),
            pltpu.VMEM((2, RING, SPAN, HD), BF16),
            pltpu.VMEM((2, RING, SPAN, HD), BF16),
            pltpu.VMEM((3, HEADS * SPAN, 2 * HD), BF16),
            pltpu.VMEM((5, HEADS * SPAN, 2 * HD), F32),
            pltpu.VMEM((5, HEADS * SPAN, HD), F32),
            pltpu.VMEM((2, SPAN, 4 * SPAN), F32),
            pltpu.VMEM((ROWS_Y, 2, SPAN, WIDE), BF16),
            pltpu.VMEM((ROWS_Y, 2, 8, 128), F32),
            pltpu.VMEM((ROWS_Y, 2, SPAN, WIDE), BF16),
            pltpu.VMEM((ROWS_Y, 2, 8, 128), F32),
            dma((ROWS_Y, 2)),
            dma((ROWS_Y, 2)),
            dma((2, 2, 2, 4)),
            dma((2, 2, 2, 4)),
            dma((ROWS_Y, 2)),
            dma((ROWS_Y, 2)),
            dma((ROWS_Y, 2)),
            dma((ROWS_Y, 2)),
        ],
        compiler_params=pltpu.CompilerParams(
            collective_id=0, has_side_effects=True, vmem_limit_bytes=48 * 2**20
        ),
    )(q.reshape(2, SPAN, WIDE), k.reshape(2, SPAN, HD), v.reshape(2, SPAN, HD))
    out = pl.pallas_call(
        lightning_kernel,
        out_shape=jax.ShapeDtypeStruct((2, SPAN, WIDE), BF16),
        in_specs=[VMEM, VMEM, VMEM, VMEM, SMEM, VMEM],
        out_specs=VMEM,
        scratch_shapes=[
            pltpu.VMEM((2, CTX, 32, HD), BF16),
            pltpu.VMEM((2, CTX, 32, HD), BF16),
            pltpu.VMEM((2, CTX, 16, HD), BF16),
            pltpu.VMEM((2, CTX, 16, HD), BF16),
            pltpu.VMEM((2, SPAN, WIDE), F32),
            pltpu.VMEM((2, SPAN, WIDE), BF16),
            pltpu.VMEM((8, 128), F32),
            pltpu.VMEM((GROUP, 8, 128), F32),
            dma,
            dma,
            dma,
            dma,
            dma((GROUP,)),
            dma((GROUP,)),
        ],
        compiler_params=pltpu.CompilerParams(
            collective_id=1, has_side_effects=True, vmem_limit_bytes=48 * 2**20
        ),
    )(
        attention,
        lq.reshape(2, SPAN, WIDE),
        lk.reshape(2, SPAN, WIDE),
        shrink.reshape(2, SPAN),
        fading,
        gain.reshape(1, WIDE),
    )
    return out.reshape(2 * SPAN, WIDE)


def solution(mesh):
    placed = (
        P("ctx", "head"),
        P("ctx", "head"),
        P("ctx", "head"),
        P("ctx", "head"),
        P("ctx", "head"),
        P("head"),
        P("ctx"),
        P("head"),
    )
    return jax.shard_map(
        per_device, mesh=mesh, in_specs=placed, out_specs=P("ctx", "head"), check_vma=False
    )
```

```python
import functools
import math

import jax
import jax.numpy as jnp
from jax import lax
from jax.experimental import pallas as pl
from jax.experimental.pallas import tpu as pltpu
from jax.sharding import PartitionSpec as P

HQ = 32
HD = 128
SPAN = 256
HEADS = 4
ROWS_Y = 4
RING = 8
CTX = 32
GROUP = 8
NORM_EPSILON = 1e-06
LOW = -1e30
MESH = pl.DeviceIdType.MESH
F32 = jnp.float32
BF16 = jnp.bfloat16
NT = (((1,), (1,)), ((), ()))
NN = (((1,), (0,)), ((), ()))
TN = (((0,), (0,)), ((), ()))


def dot(a, b, dims=NN):
    return lax.dot_general(a, b, dims, preferred_element_type=F32)


def eye_mask():
    return lax.broadcasted_iota(jnp.int32, (128, 128), 0) == lax.broadcasted_iota(
        jnp.int32, (128, 128), 1
    )


def column_to_row(column):
    return jnp.sum(jnp.where(eye_mask(), column, 0.0), axis=0, keepdims=True)


def row_to_column(row):
    spread = jnp.where(eye_mask(), jnp.broadcast_to(row, (128, 128)), 0.0)
    return jnp.broadcast_to(jnp.sum(spread, axis=1, keepdims=True), (128, 128))


def twice(x):
    return jnp.concatenate([x, x], axis=1)


def split_queries(source, target):
    scale = math.log2(math.e) / math.sqrt(HD)
    for h in range(HEADS):
        scaled = source[:, h * HD : (h + 1) * HD].astype(F32) * scale
        high = scaled.astype(BF16)
        low = (scaled - high.astype(F32)).astype(BF16)
        target[h * SPAN : (h + 1) * SPAN, 0:HD] = high
        target[h * SPAN : (h + 1) * SPAN, HD : 2 * HD] = low


def attend(items, scores):
    def product(item, h, slot):
        queries, keys, _, size, _, _, masked = item
        k = twice(keys[...].reshape(size, HD))
        s = dot(queries[h * SPAN : (h + 1) * SPAN, :], k, NT)
        if masked:
            row = lax.broadcasted_iota(jnp.int32, (SPAN, size), 0)
            col = lax.broadcasted_iota(jnp.int32, (SPAN, size), 1)
            s = jnp.where(col <= row, s, LOW)
        scores[slot, :, 0:size] = s

    def fold(item, h, slot):
        _, _, values, size, accum, highest, _ = item
        rows = slice(h * SPAN, (h + 1) * SPAN)
        s = scores[slot, :, 0:size]
        old = highest[rows, :]
        new = jnp.maximum(
            old, jnp.broadcast_to(jnp.max(s, axis=1, keepdims=True), (SPAN, HD))
        )
        factor = jnp.exp2(old - new)
        p = jnp.exp2(s - jnp.concatenate([new] * (size // HD), axis=1)).astype(BF16)
        v = values[...].reshape(size, HD)
        v = jnp.concatenate([v, jnp.ones_like(v)], axis=1)
        accum[rows, :] = accum[rows, :] * twice(factor) + dot(p, v)
        highest[rows, :] = new

    steps = [(item, h) for item in items for h in range(HEADS)]
    product(*steps[0], 0)
    for n, step in enumerate(steps):
        if n + 1 < len(steps):
            product(*steps[n + 1], (n + 1) % 2)
        fold(*step, n % 2)


def kernel(
    q_ref, k_ref, v_ref, lq_ref, lk_ref, shrink_ref, fading_ref, gain_ref, out_ref,
    qbuf, kbuf, vbuf, qs, accum, highest, scores, osend, lsend, orecv, lrecv,
    lq, lk, shrink_buf, mixer, decayed, kd, qd, mixed,
    decay, scan_state, usend, urecv, ssend, srecv, sqsend, sqrecv,
    load_sem, qsend_sem, qrecv_sem, kvsend_sem, kvrecv_sem, osend_sem, orecv_sem,
    lsend_sem, lrecv_sem, usend_sem, urecv_sem, ssend_sem, srecv_sem,
    sqsend_sem, sqrecv_sem,
):
    me = lax.axis_index("ctx")
    head = lax.axis_index("head")
    y, z = me // RING, lax.rem(me, RING)
    right = y * RING + lax.rem(z + 1, RING)
    left = y * RING + lax.rem(z + RING - 1, RING)

    def row_of(r):
        return lax.rem(y + r, ROWS_Y)

    def partner(r):
        return row_of(r) * RING + z

    loads = [
        pltpu.make_async_copy(source, target, load_sem.at[n])
        for n, (source, target) in enumerate(
            (
                (q_ref, qbuf.at[0]),
                (k_ref, kbuf.at[:, 0]),
                (v_ref, vbuf.at[:, 0]),
                (shrink_ref.at[pl.ds(0, SPAN)], shrink_buf.at[0]),
                (shrink_ref.at[pl.ds(SPAN, SPAN)], shrink_buf.at[1]),
                (lq_ref, lq),
                (lk_ref, lk),
            )
        )
    ]
    for load in loads:
        load.start()

    barrier = pltpu.get_barrier_semaphore()

    @pl.loop(1, CTX)
    def _(k):
        pl.semaphore_signal(
            barrier, inc=1, device_id={"ctx": lax.rem(me + k, CTX)}, device_id_type=MESH
        )

    @pl.loop(1, GROUP)
    def _(k):
        pl.semaphore_signal(
            barrier, inc=1, device_id={"head": lax.rem(head + k, GROUP)}, device_id_type=MESH
        )

    pl.semaphore_wait(barrier, CTX - 1 + GROUP - 1)

    def ring_copy(half, way, piece, s):
        buf, own = (kbuf, k_ref) if piece == 0 else (vbuf, v_ref)
        target = 1 if s == 3 else 2 * (s + 1) + way
        src = own.at[half] if s == 0 else buf.at[half, 2 * s + way]
        return pltpu.make_async_remote_copy(
            src_ref=src,
            dst_ref=buf.at[half, target],
            send_sem=kvsend_sem.at[half, way, piece, s],
            recv_sem=kvrecv_sem.at[half, way, piece, s],
            device_id={"ctx": right if way == 0 else left},
            device_id_type=MESH,
        )

    def pieces(way, s):
        return (0, 1) if s < 3 else (way,)

    def ring_send(half, s):
        for piece in (0, 1):
            for way in (0, 1):
                if piece in pieces(way, s):
                    ring_copy(half, way, piece, s).start()

    def ring_step(half, s):
        for piece in (0, 1):
            for way in (0, 1):
                if piece in pieces(way, s - 1):
                    ring_copy(half, way, piece, s - 1).wait_recv()
                if s < 4 and piece in pieces(way, s):
                    ring_copy(half, way, piece, s).start()

    def query_copy(r, half, slot=None):
        slot = ROWS_Y - r if slot is None else slot
        return pltpu.make_async_remote_copy(
            src_ref=q_ref.at[half],
            dst_ref=qbuf.at[slot, half],
            send_sem=qsend_sem.at[r, half],
            recv_sem=qrecv_sem.at[slot, half],
            device_id={"ctx": partner(r)},
            device_id_type=MESH,
        )

    def result_copies(r, half, slot=None):
        slot = ROWS_Y - r if slot is None else slot
        return (
            pltpu.make_async_remote_copy(
                src_ref=osend.at[r, half],
                dst_ref=orecv.at[slot, half],
                send_sem=osend_sem.at[r, half],
                recv_sem=orecv_sem.at[slot, half],
                device_id={"ctx": partner(r)},
                device_id_type=MESH,
            ),
            pltpu.make_async_remote_copy(
                src_ref=lsend.at[r, half],
                dst_ref=lrecv.at[slot, half],
                send_sem=lsend_sem.at[r, half],
                recv_sem=lrecv_sem.at[slot, half],
                device_id={"ctx": partner(r)},
                device_id_type=MESH,
            ),
        )

    def spread_copy(source, target, send_sem, recv_sem, k):
        other = lax.rem(me + k, CTX)
        return pltpu.make_async_remote_copy(
            src_ref=source(other),
            dst_ref=target(me),
            send_sem=send_sem,
            recv_sem=recv_sem,
            device_id={"ctx": other},
            device_id_type=MESH,
        )

    def spread_all(whole_source, whole_target, send_sem, recv_sem):
        return pltpu.make_async_remote_copy(
            src_ref=whole_source,
            dst_ref=whole_target,
            send_sem=send_sem,
            recv_sem=recv_sem,
            device_id={"ctx": lax.rem(me + 1, CTX)},
            device_id_type=MESH,
        )

    def message(c):
        return pl.ds(0, 32 if c == 0 else 16)

    def update_all(c):
        return spread_all(
            usend.at[c, 0 : CTX - 1, message(c)], urecv.at[c, 0 : CTX - 1, message(c)],
            usend_sem.at[c], urecv_sem.at[c],
        )

    def state_all(c):
        return spread_all(
            ssend.at[c, 0 : CTX - 1], srecv.at[c, 0 : CTX - 1], ssend_sem.at[c], srecv_sem.at[c]
        )

    def send_queries(r, stage):
        if stage == 0:

            @pl.when(y > row_of(r))
            def _():
                query_copy(r, 0).start()

            @pl.when(y < row_of(r))
            def _():
                query_copy(r, 1).start()

        else:

            @pl.when(y > row_of(r))
            def _():
                query_copy(r, 1).start()

    ring_send(0, 0)
    send_queries(3, 0)
    send_queries(1, 0)

    def clear(a):
        accum[a] = jnp.zeros((HEADS * SPAN, 2 * HD), F32)
        highest[a] = jnp.full((HEADS * SPAN, HD), LOW, F32)

    def single(half, slot, masked=False):
        return (
            qs.at[half], kbuf.at[half, slot], vbuf.at[half, slot], SPAN,
            accum.at[half], highest.at[half], masked,
        )

    def pair(a, s):
        return (
            qs.at[a], kbuf.at[0, 2 * s : 2 * s + 2], vbuf.at[0, 2 * s : 2 * s + 2], 2 * SPAN,
            accum.at[a], highest.at[a], False,
        )

    def prepare(c):
        row = lax.broadcasted_iota(jnp.int32, (SPAN, SPAN), 0)
        col = lax.broadcasted_iota(jnp.int32, (SPAN, SPAN), 1)
        lower = col <= row
        step_col = (lax.broadcasted_iota(jnp.int32, (SPAN, HD), 0) + 1).astype(F32)
        step_row = (lax.broadcasted_iota(jnp.int32, (8, SPAN), 1) + 1).astype(F32)
        shrink = shrink_buf[c : c + 1, :].astype(F32)
        counts_col = jnp.broadcast_to(
            jnp.sum(
                jnp.where(lower, jnp.broadcast_to(shrink, (SPAN, SPAN)), 0.0),
                axis=1, keepdims=True,
            ),
            (SPAN, HD),
        )
        counts_row = dot(
            jnp.broadcast_to(shrink, (8, SPAN)).astype(BF16),
            jnp.where(row <= col, 1.0, 0.0).astype(BF16),
        )
        for h in range(HEADS):
            cols = slice(h * HD, (h + 1) * HD)
            power = fading_ref[h].astype(F32)
            run_col = -jnp.exp2(jnp.full((SPAN, HD), -power, F32)) * step_col - 0.5 * counts_col
            run_row = -jnp.exp2(jnp.full((8, SPAN), -power, F32)) * step_row - 0.5 * counts_row
            last = run_col[SPAN - 1 : SPAN, :]
            q = lq[c, :, cols]
            k = lk[c, :, cols]
            gap = jnp.minimum(
                twice(run_col) - jnp.broadcast_to(run_row[0:1, :], (SPAN, SPAN)), 0.0
            )
            decayed[c, h] = jnp.where(lower, dot(q, k, NT) * jnp.exp(gap), 0.0).astype(BF16)
            qd[c, :, cols] = (q.astype(F32) * jnp.exp(run_col)).astype(BF16)
            kd[c, :, cols] = (k.astype(F32) * jnp.exp(last - run_col)).astype(BF16)

    def receive_queries(r):
        above = row_of(r) > y

        @pl.when(above)
        def _():
            query_copy(r, 0, r).wait_recv()

        @pl.when(jnp.logical_not(above))
        def _():
            query_copy(r, 1, r).wait_recv()

        split_queries(qbuf.at[r, jnp.where(above, 0, 1)], qs.at[1 + r])
        clear(1 + r)

    def stream(half, a):
        @pl.loop(0, 2)
        def _(c):
            item = (
                qs.at[a], kbuf.at[half, pl.ds(4 * c, 4)], vbuf.at[half, pl.ds(4 * c, 4)],
                4 * SPAN, accum.at[a], highest.at[a], False,
            )
            attend([item], scores)

    def emit(r, half):
        a = 1 + r
        for h in range(HEADS):
            rows = slice(h * SPAN, (h + 1) * SPAN)
            total = accum[a, rows, HD : 2 * HD]
            osend[r, half, :, h * HD : (h + 1) * HD] = (accum[a, rows, 0:HD] / total).astype(BF16)
            level = highest[a, rows, :] + jnp.log2(total)
            for g in range(2):
                lsend[r, half, 2 * h + g : 2 * h + g + 1, :] = column_to_row(
                    level[g * 128 : (g + 1) * 128, :]
                )
        for copy in result_copies(r, half):
            copy.start()

    def combine(half):
        for r in (1, 2, 3):
            if half == 1:
                for copy in result_copies(r, 1, r):
                    copy.wait_recv()
            else:
                below = row_of(r) < y

                @pl.when(below)
                def _(r=r):
                    for copy in result_copies(r, 0, r):
                        copy.wait_recv()

                @pl.when(jnp.logical_not(below))
                def _(r=r):
                    orecv[r, 0] = jnp.zeros((SPAN, HEADS * HD), BF16)
                    lrecv[r, 0] = jnp.full((8, 128), LOW, F32)

        for h in range(HEADS):
            for g in range(2):
                rows = slice(h * SPAN + g * 128, h * SPAN + (g + 1) * 128)
                part = slice(g * 128, (g + 1) * 128)
                cols = slice(h * HD, (h + 1) * HD)
                total = accum[half, rows, HD : 2 * HD]
                levels = [highest[half, rows, :] + jnp.log2(total)]
                values = [accum[half, rows, 0:HD] / total]
                for r in (1, 2, 3):
                    levels.append(row_to_column(lrecv[r, half, 2 * h + g : 2 * h + g + 1, :]))
                    values.append(orecv[r, half, part, cols].astype(F32))
                top = functools.reduce(jnp.maximum, levels)
                weights = [jnp.exp2(level - top) for level in levels]
                value = sum(w * v for w, v in zip(weights, values)) / sum(weights)
                mixer[half, part, cols] = value.astype(BF16)

    def send_updates(c):
        for h in range(HEADS):
            cols = slice(h * HD, (h + 1) * HD)
            update = dot(kd[c, :, cols], mixer[c, :, cols], TN).astype(BF16)
            usend[c, 8 * h : 8 * h + 8, 0:16] = update.reshape(8, 16, HD)
        if c == 0:
            counts = [
                jnp.broadcast_to(
                    jnp.sum(shrink_buf[n : n + 1, :].astype(F32), axis=1, keepdims=True), (8, HD)
                )
                for n in (0, 1)
            ]
            both = jnp.concatenate(counts, axis=0).astype(BF16)
            for n in range(CTX):
                usend[0, n, 16:32] = both

        @pl.loop(1, CTX)
        def _(k):
            spread_copy(
                lambda other: usend.at[c, other, message(c)],
                lambda mine: urecv.at[c, mine, message(c)],
                usend_sem.at[c], urecv_sem.at[c], k,
            ).start()

        urecv[c, me, message(c)] = usend[c, me, message(c)]
        for h in range(HEADS):
            cols = slice(h * HD, (h + 1) * HD)
            mixed[c, :, cols] = dot(decayed[c, h], mixer[c, :, cols])

    def scan(c):
        update_all(c).wait_recv()
        if c == 0:
            power = fading_ref[me // 8].astype(F32)
            block_step = SPAN * jnp.exp2(jnp.full((8, HD), -power, F32))
            for b in range(CTX):
                counts = urecv[0, b, 16:32].astype(F32)
                for n in (0, 1):
                    decay[n, b] = jnp.exp(-block_step - 0.5 * counts[8 * n : 8 * n + 8, :])
        state = jnp.zeros((16, HD), F32) if c == 0 else scan_state[...]
        for b in range(CTX) if c == 0 else reversed(range(CTX)):
            ssend[c, b] = state.astype(BF16)
            factor = decay[c, b]
            factor = jnp.concatenate([factor, factor], axis=0)
            state = factor * state + urecv[c, b, 0:16].astype(F32)
        if c == 0:
            scan_state[...] = state

        @pl.loop(1, CTX)
        def _(k):
            spread_copy(
                lambda other: ssend.at[c, other], lambda mine: srecv.at[c, mine],
                ssend_sem.at[c], srecv_sem.at[c], k,
            ).start()

        srecv[c, me] = ssend[c, me]

    def square_copy(c, k):
        return pltpu.make_async_remote_copy(
            src_ref=sqsend.at[c],
            dst_ref=sqrecv.at[c, GROUP - k],
            send_sem=sqsend_sem.at[c, k],
            recv_sem=sqrecv_sem.at[c, GROUP - k],
            device_id={"head": lax.rem(head + k, GROUP)},
            device_id_type=MESH,
        )

    def add_states(c):
        state_all(c).wait_recv()
        squares = jnp.zeros((SPAN, HD), F32)
        for h in range(HEADS):
            cols = slice(h * HD, (h + 1) * HD)
            state_h = srecv[c, 8 * h : 8 * h + 8].reshape(HD, HD)
            value = mixed[c, :, cols] + dot(qd[c, :, cols], state_h)
            mixed[c, :, cols] = value
            squares = squares + value * value
        column = jnp.broadcast_to(jnp.sum(squares, axis=1, keepdims=True), (SPAN, HD))
        sqsend[c] = jnp.zeros((8, 128), F32)
        for g in range(2):
            sqsend[c, g : g + 1, :] = column_to_row(column[g * 128 : (g + 1) * 128, :])
        for k in range(1, GROUP):
            square_copy(c, k).start()

    def finish(c):
        total = sqsend[c]
        for k in range(1, GROUP):
            square_copy(c, k).wait_recv()
        for k in range(1, GROUP):
            total = total + sqrecv[c, k]
        scale = lax.rsqrt(total * (1.0 / (HQ * HD)) + NORM_EPSILON)
        for g in range(2):
            column = row_to_column(scale[g : g + 1, :])
            part = slice(g * 128, (g + 1) * 128)
            for h in range(HEADS):
                cols = slice(h * HD, (h + 1) * HD)
                gain = jnp.broadcast_to(gain_ref[0:1, cols].astype(F32), (128, HD))
                out_ref[c, part, cols] = (mixed[c, part, cols] * column * gain).astype(BF16)

    def first_results(r):
        @pl.when(row_of(r) > y)
        def _():
            emit(r, 0)

    def second_job(r):
        above = row_of(r) > y

        @pl.when(above)
        def _():
            query_copy(r, 1, r).wait_recv()
            split_queries(qbuf.at[r, 1], qs.at[1 + r])
            clear(1 + r)

        stream(jnp.where(above, 0, 1), 1 + r)
        emit(r, 1)

    def singles(slots):
        items = []
        for slot in slots:
            away = 4 if slot == 1 else (RING - slot // 2 if slot % 2 == 0 else slot // 2)
            items.append(single(jnp.where(lax.rem(z + away, RING) < z, 0, 1), slot))
        return items

    for n in range(3):
        loads[n].wait()
    for half in (0, 1):
        split_queries(qbuf.at[0, half], qs.at[half])
        clear(half)
    attend([single(0, 0, True), single(1, 0, True)], scores)
    for n in range(3, len(loads)):
        loads[n].wait()
    prepare(0)
    ring_step(0, 1)
    send_queries(2, 0)
    attend([pair(1, 1)], scores)
    prepare(1)
    ring_step(0, 2)
    ring_send(1, 0)
    receive_queries(3)
    receive_queries(1)
    attend([pair(4, 1), pair(2, 1), pair(4, 2), pair(2, 2)], scores)
    ring_step(0, 3)
    for r in (1, 2, 3):
        send_queries(r, 1)
    attend([pair(4, 3), pair(2, 3), pair(1, 2)], scores)
    ring_step(0, 4)
    ring_step(1, 1)
    attend([pair(4, 0), pair(2, 0)], scores)
    first_results(3)
    first_results(1)
    ring_step(1, 2)
    receive_queries(2)
    stream(0, 3)
    first_results(2)
    ring_step(1, 3)
    for r in (1, 2):
        pl.when(y == ROWS_Y - r)(lambda: ring_step(1, 4))
        second_job(r)
    pl.when(y < 2)(lambda: ring_step(1, 4))
    attend(singles((2, 3, 4, 5, 6, 7, 1)), scores)
    combine(0)
    send_updates(0)
    second_job(3)
    attend([pair(1, 3), pair(1, 0)], scores)
    scan(0)
    combine(1)
    send_updates(1)
    add_states(0)
    scan(1)
    finish(0)
    add_states(1)
    finish(1)

    for half in (0, 1):
        for s in range(4):
            for way in (0, 1):
                for piece in pieces(way, s):
                    ring_copy(half, way, piece, s).wait_send()
    for r in (1, 2, 3):

        @pl.when(y > row_of(r))
        def _(r=r):
            query_copy(r, 0).wait_send()

        query_copy(r, 1).wait_send()

        @pl.when(row_of(r) > y)
        def _(r=r):
            for copy in result_copies(r, 0):
                copy.wait_send()

        for copy in result_copies(r, 1):
            copy.wait_send()
    for c in (0, 1):
        update_all(c).wait_send()
        state_all(c).wait_send()
        for k in range(1, GROUP):
            square_copy(c, k).wait_send()


WIDE = HEADS * HD


def per_device(q, k, v, lq, lk, fading, shrink, gain):
    dma = pltpu.SemaphoreType.DMA
    anywhere = pl.BlockSpec(memory_space=pl.ANY)
    vmem = pltpu.VMEM
    out = pl.pallas_call(
        kernel,
        out_shape=jax.ShapeDtypeStruct((2, SPAN, WIDE), BF16),
        in_specs=[anywhere] * 6
        + [pl.BlockSpec(memory_space=pltpu.SMEM), pl.BlockSpec(memory_space=pltpu.VMEM)],
        out_specs=pl.BlockSpec(memory_space=pltpu.VMEM),
        scratch_shapes=[
            vmem((ROWS_Y, 2, SPAN, WIDE), BF16),
            vmem((2, RING, SPAN, HD), BF16),
            vmem((2, RING, SPAN, HD), BF16),
            vmem((5, HEADS * SPAN, 2 * HD), BF16),
            vmem((5, HEADS * SPAN, 2 * HD), F32),
            vmem((5, HEADS * SPAN, HD), F32),
            vmem((2, SPAN, 4 * SPAN), F32),
            vmem((ROWS_Y, 2, SPAN, WIDE), BF16),
            vmem((ROWS_Y, 2, 8, 128), F32),
            vmem((ROWS_Y, 2, SPAN, WIDE), BF16),
            vmem((ROWS_Y, 2, 8, 128), F32),
            vmem((2, SPAN, WIDE), BF16),
            vmem((2, SPAN, WIDE), BF16),
            vmem((2, SPAN), jnp.int32),
            vmem((2, SPAN, WIDE), BF16),
            vmem((2, HEADS, SPAN, SPAN), BF16),
            vmem((2, SPAN, WIDE), BF16),
            vmem((2, SPAN, WIDE), BF16),
            vmem((2, SPAN, WIDE), F32),
            vmem((2, CTX, 8, HD), F32),
            vmem((16, HD), F32),
            vmem((2, CTX, 32, HD), BF16),
            vmem((2, CTX, 32, HD), BF16),
            vmem((2, CTX, 16, HD), BF16),
            vmem((2, CTX, 16, HD), BF16),
            vmem((2, 8, 128), F32),
            vmem((2, GROUP, 8, 128), F32),
            dma((7,)),
            dma((ROWS_Y, 2)),
            dma((ROWS_Y, 2)),
            dma((2, 2, 2, 4)),
            dma((2, 2, 2, 4)),
            dma((ROWS_Y, 2)),
            dma((ROWS_Y, 2)),
            dma((ROWS_Y, 2)),
            dma((ROWS_Y, 2)),
            dma((2,)),
            dma((2,)),
            dma((2,)),
            dma((2,)),
            dma((2, GROUP)),
            dma((2, GROUP)),
        ],
        compiler_params=pltpu.CompilerParams(
            collective_id=0, has_side_effects=True, vmem_limit_bytes=56 * 2**20
        ),
    )(
        q.reshape(2, SPAN, WIDE),
        k.reshape(2, SPAN, HD),
        v.reshape(2, SPAN, HD),
        lq.reshape(2, SPAN, WIDE),
        lk.reshape(2, SPAN, WIDE),
        shrink,
        fading,
        gain.reshape(1, WIDE),
    )
    return out.reshape(2 * SPAN, WIDE)


def solution(mesh):
    placed = (
        P("ctx", "head"),
        P("ctx", "head"),
        P("ctx", "head"),
        P("ctx", "head"),
        P("ctx", "head"),
        P("head"),
        P("ctx"),
        P("head"),
    )
    return jax.shard_map(
        per_device, mesh=mesh, in_specs=placed, out_specs=P("ctx", "head"), check_vma=False
    )
```

```python
import functools
import math

import jax
import jax.numpy as jnp
from jax import lax
from jax.experimental import pallas as pl
from jax.experimental.pallas import tpu as pltpu
from jax.sharding import PartitionSpec as P

HQ = 32
HD = 128
SPAN = 256
HEADS = 4
ROWS_Y = 4
RING = 8
CTX = 32
GROUP = 8
NORM_EPSILON = 1e-06
LOW = -1e30
MESH = pl.DeviceIdType.MESH
F32 = jnp.float32
BF16 = jnp.bfloat16
NT = (((1,), (1,)), ((), ()))
NN = (((1,), (0,)), ((), ()))
TN = (((0,), (0,)), ((), ()))


def dot(a, b, dims=NN):
    return lax.dot_general(a, b, dims, preferred_element_type=F32)


def eye_mask():
    return lax.broadcasted_iota(jnp.int32, (128, 128), 0) == lax.broadcasted_iota(
        jnp.int32, (128, 128), 1
    )


def column_to_row(column):
    return jnp.sum(jnp.where(eye_mask(), column, 0.0), axis=0, keepdims=True)


def row_to_column(row):
    spread = jnp.where(eye_mask(), jnp.broadcast_to(row, (128, 128)), 0.0)
    return jnp.broadcast_to(jnp.sum(spread, axis=1, keepdims=True), (128, 128))


def twice(x):
    return jnp.concatenate([x, x], axis=1)


def split_queries(source, target):
    scale = math.log2(math.e) / math.sqrt(HD)
    for h in range(HEADS):
        scaled = source[:, h * HD : (h + 1) * HD].astype(F32) * scale
        high = scaled.astype(BF16)
        low = (scaled - high.astype(F32)).astype(BF16)
        target[h * SPAN : (h + 1) * SPAN, 0:HD] = high
        target[h * SPAN : (h + 1) * SPAN, HD : 2 * HD] = low


def attend(items, scores):
    def product(item, h, slot):
        queries, keys, _, size, _, _, masked = item
        k = twice(keys[...].reshape(size, HD))
        s = dot(queries[h * SPAN : (h + 1) * SPAN, :], k, NT)
        if masked:
            row = lax.broadcasted_iota(jnp.int32, (SPAN, size), 0)
            col = lax.broadcasted_iota(jnp.int32, (SPAN, size), 1)
            s = jnp.where(col <= row, s, LOW)
        scores[slot, :, 0:size] = s

    def fold(item, h, slot):
        _, _, values, size, accum, highest, _ = item
        rows = slice(h * SPAN, (h + 1) * SPAN)
        s = scores[slot, :, 0:size]
        old = highest[rows, :]
        new = jnp.maximum(
            old, jnp.broadcast_to(jnp.max(s, axis=1, keepdims=True), (SPAN, HD))
        )
        factor = jnp.exp2(old - new)
        p = jnp.exp2(s - jnp.concatenate([new] * (size // HD), axis=1)).astype(BF16)
        v = values[...].reshape(size, HD)
        v = jnp.concatenate([v, jnp.ones_like(v)], axis=1)
        accum[rows, :] = accum[rows, :] * twice(factor) + dot(p, v)
        highest[rows, :] = new

    steps = [(item, h) for item in items for h in range(HEADS)]
    product(*steps[0], 0)
    for n, step in enumerate(steps):
        if n + 1 < len(steps):
            product(*steps[n + 1], (n + 1) % 2)
        fold(*step, n % 2)


def kernel(
    q_ref, k_ref, v_ref, lq_ref, lk_ref, shrink_ref, fading_ref, gain_ref, out_ref,
    qbuf, kbuf, vbuf, qs, accum, highest, scores, osend, lsend, orecv, lrecv,
    lq, lk, shrink_buf, mixer, decayed, kd, qd, mixed,
    decay, scan_state, usend, urecv, ssend, srecv, sqsend, sqrecv,
    load_sem, qsend_sem, qrecv_sem, kvsend_sem, kvrecv_sem, osend_sem, orecv_sem,
    lsend_sem, lrecv_sem, usend_sem, urecv_sem, ssend_sem, srecv_sem,
    sqsend_sem, sqrecv_sem,
):
    me = lax.axis_index("ctx")
    head = lax.axis_index("head")
    y, z = me // RING, lax.rem(me, RING)
    right = y * RING + lax.rem(z + 1, RING)
    left = y * RING + lax.rem(z + RING - 1, RING)

    def row_of(r):
        return lax.rem(y + r, ROWS_Y)

    def partner(r):
        return row_of(r) * RING + z

    loads = [
        pltpu.make_async_copy(source, target, load_sem.at[n])
        for n, (source, target) in enumerate(
            (
                (q_ref, qbuf.at[0]),
                (k_ref, kbuf.at[:, 0]),
                (v_ref, vbuf.at[:, 0]),
                (shrink_ref.at[pl.ds(0, SPAN)], shrink_buf.at[0]),
                (shrink_ref.at[pl.ds(SPAN, SPAN)], shrink_buf.at[1]),
                (lq_ref, lq),
                (lk_ref, lk),
            )
        )
    ]
    for load in loads:
        load.start()

    barrier = pltpu.get_barrier_semaphore()

    @pl.loop(1, CTX)
    def _(k):
        pl.semaphore_signal(
            barrier, inc=1, device_id={"ctx": lax.rem(me + k, CTX)}, device_id_type=MESH
        )

    @pl.loop(1, GROUP)
    def _(k):
        pl.semaphore_signal(
            barrier, inc=1, device_id={"head": lax.rem(head + k, GROUP)}, device_id_type=MESH
        )

    pl.semaphore_wait(barrier, CTX - 1 + GROUP - 1)

    def ring_copy(half, way, piece, s):
        buf, own = (kbuf, k_ref) if piece == 0 else (vbuf, v_ref)
        target = 1 if s == 3 else 2 * (s + 1) + way
        src = own.at[half] if s == 0 else buf.at[half, 2 * s + way]
        return pltpu.make_async_remote_copy(
            src_ref=src,
            dst_ref=buf.at[half, target],
            send_sem=kvsend_sem.at[half, way, piece, s],
            recv_sem=kvrecv_sem.at[half, way, piece, s],
            device_id={"ctx": right if way == 0 else left},
            device_id_type=MESH,
        )

    def pieces(way, s):
        return (0, 1) if s < 3 else (way,)

    def ring_send(half, s):
        for piece in (0, 1):
            for way in (0, 1):
                if piece in pieces(way, s):
                    ring_copy(half, way, piece, s).start()

    def ring_step(half, s):
        for piece in (0, 1):
            for way in (0, 1):
                if piece in pieces(way, s - 1):
                    ring_copy(half, way, piece, s - 1).wait_recv()
                if s < 4 and piece in pieces(way, s):
                    ring_copy(half, way, piece, s).start()

    def query_copy(r, half, slot=None):
        slot = ROWS_Y - r if slot is None else slot
        return pltpu.make_async_remote_copy(
            src_ref=q_ref.at[half],
            dst_ref=qbuf.at[slot, half],
            send_sem=qsend_sem.at[r, half],
            recv_sem=qrecv_sem.at[slot, half],
            device_id={"ctx": partner(r)},
            device_id_type=MESH,
        )

    def result_copies(r, half, slot=None):
        slot = ROWS_Y - r if slot is None else slot
        return (
            pltpu.make_async_remote_copy(
                src_ref=osend.at[r, half],
                dst_ref=orecv.at[slot, half],
                send_sem=osend_sem.at[r, half],
                recv_sem=orecv_sem.at[slot, half],
                device_id={"ctx": partner(r)},
                device_id_type=MESH,
            ),
            pltpu.make_async_remote_copy(
                src_ref=lsend.at[r, half],
                dst_ref=lrecv.at[slot, half],
                send_sem=lsend_sem.at[r, half],
                recv_sem=lrecv_sem.at[slot, half],
                device_id={"ctx": partner(r)},
                device_id_type=MESH,
            ),
        )

    def spread_copy(source, target, send_sem, recv_sem, k):
        other = lax.rem(me + k, CTX)
        return pltpu.make_async_remote_copy(
            src_ref=source(other),
            dst_ref=target(me),
            send_sem=send_sem,
            recv_sem=recv_sem,
            device_id={"ctx": other},
            device_id_type=MESH,
        )

    def spread_all(whole_source, whole_target, send_sem, recv_sem):
        return pltpu.make_async_remote_copy(
            src_ref=whole_source,
            dst_ref=whole_target,
            send_sem=send_sem,
            recv_sem=recv_sem,
            device_id={"ctx": lax.rem(me + 1, CTX)},
            device_id_type=MESH,
        )

    def message(c):
        return pl.ds(0, 32 if c == 0 else 16)

    def update_all(c):
        return spread_all(
            usend.at[c, 0 : CTX - 1, message(c)], urecv.at[c, 0 : CTX - 1, message(c)],
            usend_sem.at[c], urecv_sem.at[c],
        )

    def state_all(c):
        return spread_all(
            ssend.at[c, 0 : CTX - 1], srecv.at[c, 0 : CTX - 1], ssend_sem.at[c], srecv_sem.at[c]
        )

    def send_queries(r, stage):
        if stage == 0:

            @pl.when(y > row_of(r))
            def _():
                query_copy(r, 0).start()

            @pl.when(y < row_of(r))
            def _():
                query_copy(r, 1).start()

        else:

            @pl.when(y > row_of(r))
            def _():
                query_copy(r, 1).start()

    ring_send(0, 0)
    send_queries(3, 0)
    send_queries(1, 0)

    def clear(a):
        accum[a] = jnp.zeros((HEADS * SPAN, 2 * HD), F32)
        highest[a] = jnp.full((HEADS * SPAN, HD), LOW, F32)

    def single(half, slot, masked=False):
        return (
            qs.at[half], kbuf.at[half, slot], vbuf.at[half, slot], SPAN,
            accum.at[half], highest.at[half], masked,
        )

    def pair(a, s):
        return (
            qs.at[a], kbuf.at[0, 2 * s : 2 * s + 2], vbuf.at[0, 2 * s : 2 * s + 2], 2 * SPAN,
            accum.at[a], highest.at[a], False,
        )

    def prepare(c):
        row = lax.broadcasted_iota(jnp.int32, (SPAN, SPAN), 0)
        col = lax.broadcasted_iota(jnp.int32, (SPAN, SPAN), 1)
        lower = col <= row
        step_col = (lax.broadcasted_iota(jnp.int32, (SPAN, HD), 0) + 1).astype(F32)
        step_row = (lax.broadcasted_iota(jnp.int32, (8, SPAN), 1) + 1).astype(F32)
        shrink = shrink_buf[c : c + 1, :].astype(F32)
        counts_col = jnp.broadcast_to(
            jnp.sum(
                jnp.where(lower, jnp.broadcast_to(shrink, (SPAN, SPAN)), 0.0),
                axis=1, keepdims=True,
            ),
            (SPAN, HD),
        )
        counts_row = dot(
            jnp.broadcast_to(shrink, (8, SPAN)).astype(BF16),
            jnp.where(row <= col, 1.0, 0.0).astype(BF16),
        )
        for h in range(HEADS):
            cols = slice(h * HD, (h + 1) * HD)
            power = fading_ref[h].astype(F32)
            run_col = -jnp.exp2(jnp.full((SPAN, HD), -power, F32)) * step_col - 0.5 * counts_col
            run_row = -jnp.exp2(jnp.full((8, SPAN), -power, F32)) * step_row - 0.5 * counts_row
            last = run_col[SPAN - 1 : SPAN, :]
            q = lq[c, :, cols]
            k = lk[c, :, cols]
            gap = jnp.minimum(
                twice(run_col) - jnp.broadcast_to(run_row[0:1, :], (SPAN, SPAN)), 0.0
            )
            decayed[c, h] = jnp.where(lower, dot(q, k, NT) * jnp.exp(gap), 0.0).astype(BF16)
            qd[c, :, cols] = (q.astype(F32) * jnp.exp(run_col)).astype(BF16)
            kd[c, :, cols] = (k.astype(F32) * jnp.exp(last - run_col)).astype(BF16)

    def receive_queries(r):
        above = row_of(r) > y

        @pl.when(above)
        def _():
            query_copy(r, 0, r).wait_recv()

        @pl.when(jnp.logical_not(above))
        def _():
            query_copy(r, 1, r).wait_recv()

        split_queries(qbuf.at[r, jnp.where(above, 0, 1)], qs.at[1 + r])
        clear(1 + r)

    def stream(half, a):
        @pl.loop(0, 2)
        def _(c):
            item = (
                qs.at[a], kbuf.at[half, pl.ds(4 * c, 4)], vbuf.at[half, pl.ds(4 * c, 4)],
                4 * SPAN, accum.at[a], highest.at[a], False,
            )
            attend([item], scores)

    def emit(r, half):
        a = 1 + r
        for h in range(HEADS):
            rows = slice(h * SPAN, (h + 1) * SPAN)
            total = accum[a, rows, HD : 2 * HD]
            osend[r, half, :, h * HD : (h + 1) * HD] = (accum[a, rows, 0:HD] / total).astype(BF16)
            level = highest[a, rows, :] + jnp.log2(total)
            for g in range(2):
                lsend[r, half, 2 * h + g : 2 * h + g + 1, :] = column_to_row(
                    level[g * 128 : (g + 1) * 128, :]
                )
        for copy in result_copies(r, half):
            copy.start()

    def combine(half):
        for r in (1, 2, 3):
            if half == 1:
                for copy in result_copies(r, 1, r):
                    copy.wait_recv()
            else:
                below = row_of(r) < y

                @pl.when(below)
                def _(r=r):
                    for copy in result_copies(r, 0, r):
                        copy.wait_recv()

                @pl.when(jnp.logical_not(below))
                def _(r=r):
                    orecv[r, 0] = jnp.zeros((SPAN, HEADS * HD), BF16)
                    lrecv[r, 0] = jnp.full((8, 128), LOW, F32)

        for h in range(HEADS):
            for g in range(2):
                rows = slice(h * SPAN + g * 128, h * SPAN + (g + 1) * 128)
                part = slice(g * 128, (g + 1) * 128)
                cols = slice(h * HD, (h + 1) * HD)
                total = accum[half, rows, HD : 2 * HD]
                levels = [highest[half, rows, :] + jnp.log2(total)]
                values = [accum[half, rows, 0:HD] / total]
                for r in (1, 2, 3):
                    levels.append(row_to_column(lrecv[r, half, 2 * h + g : 2 * h + g + 1, :]))
                    values.append(orecv[r, half, part, cols].astype(F32))
                top = functools.reduce(jnp.maximum, levels)
                weights = [jnp.exp2(level - top) for level in levels]
                value = sum(w * v for w, v in zip(weights, values)) / sum(weights)
                mixer[half, part, cols] = value.astype(BF16)

    def send_updates(c):
        for h in range(HEADS):
            cols = slice(h * HD, (h + 1) * HD)
            update = dot(kd[c, :, cols], mixer[c, :, cols], TN).astype(BF16)
            usend[c, 8 * h : 8 * h + 8, 0:16] = update.reshape(8, 16, HD)
        if c == 0:
            counts = [
                jnp.broadcast_to(
                    jnp.sum(shrink_buf[n : n + 1, :].astype(F32), axis=1, keepdims=True), (8, HD)
                )
                for n in (0, 1)
            ]
            both = jnp.concatenate(counts, axis=0).astype(BF16)
            for n in range(CTX):
                usend[0, n, 16:32] = both

        @pl.loop(1, CTX)
        def _(k):
            spread_copy(
                lambda other: usend.at[c, other, message(c)],
                lambda mine: urecv.at[c, mine, message(c)],
                usend_sem.at[c], urecv_sem.at[c], k,
            ).start()

        urecv[c, me, message(c)] = usend[c, me, message(c)]
        for h in range(HEADS):
            cols = slice(h * HD, (h + 1) * HD)
            mixed[c, :, cols] = dot(decayed[c, h], mixer[c, :, cols])

    def scan(c):
        update_all(c).wait_recv()
        if c == 0:
            power = fading_ref[me // 8].astype(F32)
            block_step = SPAN * jnp.exp2(jnp.full((8, HD), -power, F32))
            for b in range(CTX):
                counts = urecv[0, b, 16:32].astype(F32)
                for n in (0, 1):
                    decay[n, b] = jnp.exp(-block_step - 0.5 * counts[8 * n : 8 * n + 8, :])
        state = jnp.zeros((16, HD), F32) if c == 0 else scan_state[...]
        for b in range(CTX) if c == 0 else reversed(range(CTX)):
            ssend[c, b] = state.astype(BF16)
            factor = decay[c, b]
            factor = jnp.concatenate([factor, factor], axis=0)
            state = factor * state + urecv[c, b, 0:16].astype(F32)
        if c == 0:
            scan_state[...] = state

        @pl.loop(1, CTX)
        def _(k):
            spread_copy(
                lambda other: ssend.at[c, other], lambda mine: srecv.at[c, mine],
                ssend_sem.at[c], srecv_sem.at[c], k,
            ).start()

        srecv[c, me] = ssend[c, me]

    def square_copy(c, k):
        return pltpu.make_async_remote_copy(
            src_ref=sqsend.at[c],
            dst_ref=sqrecv.at[c, GROUP - k],
            send_sem=sqsend_sem.at[c, k],
            recv_sem=sqrecv_sem.at[c, GROUP - k],
            device_id={"head": lax.rem(head + k, GROUP)},
            device_id_type=MESH,
        )

    def add_states(c):
        state_all(c).wait_recv()
        squares = jnp.zeros((SPAN, HD), F32)
        for h in range(HEADS):
            cols = slice(h * HD, (h + 1) * HD)
            state_h = srecv[c, 8 * h : 8 * h + 8].reshape(HD, HD)
            value = mixed[c, :, cols] + dot(qd[c, :, cols], state_h)
            mixed[c, :, cols] = value
            squares = squares + value * value
        column = jnp.broadcast_to(jnp.sum(squares, axis=1, keepdims=True), (SPAN, HD))
        sqsend[c] = jnp.zeros((8, 128), F32)
        for g in range(2):
            sqsend[c, g : g + 1, :] = column_to_row(column[g * 128 : (g + 1) * 128, :])
        for k in range(1, GROUP):
            square_copy(c, k).start()

    def finish(c):
        total = sqsend[c]
        for k in range(1, GROUP):
            square_copy(c, k).wait_recv()
        for k in range(1, GROUP):
            total = total + sqrecv[c, k]
        scale = lax.rsqrt(total * (1.0 / (HQ * HD)) + NORM_EPSILON)
        for g in range(2):
            column = row_to_column(scale[g : g + 1, :])
            part = slice(g * 128, (g + 1) * 128)
            for h in range(HEADS):
                cols = slice(h * HD, (h + 1) * HD)
                gain = jnp.broadcast_to(gain_ref[0:1, cols].astype(F32), (128, HD))
                out_ref[c, part, cols] = (mixed[c, part, cols] * column * gain).astype(BF16)

    def first_results(r):
        @pl.when(row_of(r) > y)
        def _():
            emit(r, 0)

    def second_queries(r):
        @pl.when(row_of(r) > y)
        def _():
            query_copy(r, 1, r).wait_recv()
            split_queries(qbuf.at[r, 1], qs.at[1 + r])
            clear(1 + r)

    def part(r, c):
        half = jnp.where(row_of(r) > y, 0, 1)
        return (
            qs.at[1 + r], kbuf.at[half, 4 * c : 4 * c + 4], vbuf.at[half, 4 * c : 4 * c + 4],
            4 * SPAN, accum.at[1 + r], highest.at[1 + r], False,
        )

    def singles(slots):
        items = []
        for slot in slots:
            away = 4 if slot == 1 else (RING - slot // 2 if slot % 2 == 0 else slot // 2)
            items.append(single(jnp.where(lax.rem(z + away, RING) < z, 0, 1), slot))
        return items

    for n in range(3):
        loads[n].wait()
    for half in (0, 1):
        split_queries(qbuf.at[0, half], qs.at[half])
        clear(half)
    attend([single(0, 0, True), single(1, 0, True)], scores)
    for n in range(3, len(loads)):
        loads[n].wait()
    prepare(0)
    ring_step(0, 1)
    send_queries(2, 0)
    attend([pair(1, 1)], scores)
    prepare(1)
    ring_step(0, 2)
    ring_send(1, 0)
    receive_queries(3)
    receive_queries(1)
    attend([pair(4, 1), pair(2, 1), pair(4, 2), pair(2, 2)], scores)
    ring_step(0, 3)
    for r in (1, 2, 3):
        send_queries(r, 1)
    attend([pair(4, 3), pair(2, 3), pair(1, 2)], scores)
    ring_step(0, 4)
    ring_step(1, 1)
    attend([pair(4, 0), pair(2, 0)], scores)
    first_results(3)
    first_results(1)
    ring_step(1, 2)
    receive_queries(2)
    stream(0, 3)
    first_results(2)
    def drain():
        for half in (0, 1):
            for s in range(4):
                for way in (0, 1):
                    for piece in pieces(way, s):
                        ring_copy(half, way, piece, s).wait_send()
        for r in (1, 2, 3):

            @pl.when(y > row_of(r))
            def _(r=r):
                query_copy(r, 0).wait_send()

            query_copy(r, 1).wait_send()

            @pl.when(row_of(r) > y)
            def _(r=r):
                for copy in result_copies(r, 0):
                    copy.wait_send()

            for copy in result_copies(r, 1):
                copy.wait_send()

    attend(singles((2, 3, 4, 5)), scores)
    ring_step(1, 3)
    second_queries(1)
    second_queries(2)
    attend([part(1, 1), part(2, 1)], scores)
    ring_step(1, 4)
    attend([part(1, 0)], scores)
    emit(1, 1)
    attend([part(2, 0)], scores)
    emit(2, 1)
    second_queries(3)
    attend([part(3, 1), part(3, 0)], scores)
    emit(3, 1)
    attend(singles((6, 7, 1)) + [pair(1, 3), pair(1, 0)], scores)
    combine(0)
    send_updates(0)
    combine(1)
    send_updates(1)
    drain()
    scan(0)
    scan(1)
    add_states(0)
    add_states(1)
    finish(0)
    finish(1)

    for c in (0, 1):
        update_all(c).wait_send()
        state_all(c).wait_send()
        for k in range(1, GROUP):
            square_copy(c, k).wait_send()


WIDE = HEADS * HD


def per_device(q, k, v, lq, lk, fading, shrink, gain):
    dma = pltpu.SemaphoreType.DMA
    anywhere = pl.BlockSpec(memory_space=pl.ANY)
    vmem = pltpu.VMEM
    out = pl.pallas_call(
        kernel,
        out_shape=jax.ShapeDtypeStruct((2, SPAN, WIDE), BF16),
        in_specs=[anywhere] * 6
        + [pl.BlockSpec(memory_space=pltpu.SMEM), pl.BlockSpec(memory_space=pltpu.VMEM)],
        out_specs=pl.BlockSpec(memory_space=pltpu.VMEM),
        scratch_shapes=[
            vmem((ROWS_Y, 2, SPAN, WIDE), BF16),
            vmem((2, RING, SPAN, HD), BF16),
            vmem((2, RING, SPAN, HD), BF16),
            vmem((5, HEADS * SPAN, 2 * HD), BF16),
            vmem((5, HEADS * SPAN, 2 * HD), F32),
            vmem((5, HEADS * SPAN, HD), F32),
            vmem((2, SPAN, 4 * SPAN), F32),
            vmem((ROWS_Y, 2, SPAN, WIDE), BF16),
            vmem((ROWS_Y, 2, 8, 128), F32),
            vmem((ROWS_Y, 2, SPAN, WIDE), BF16),
            vmem((ROWS_Y, 2, 8, 128), F32),
            vmem((2, SPAN, WIDE), BF16),
            vmem((2, SPAN, WIDE), BF16),
            vmem((2, SPAN), jnp.int32),
            vmem((2, SPAN, WIDE), BF16),
            vmem((2, HEADS, SPAN, SPAN), BF16),
            vmem((2, SPAN, WIDE), BF16),
            vmem((2, SPAN, WIDE), BF16),
            vmem((2, SPAN, WIDE), F32),
            vmem((2, CTX, 8, HD), F32),
            vmem((16, HD), F32),
            vmem((2, CTX, 32, HD), BF16),
            vmem((2, CTX, 32, HD), BF16),
            vmem((2, CTX, 16, HD), BF16),
            vmem((2, CTX, 16, HD), BF16),
            vmem((2, 8, 128), F32),
            vmem((2, GROUP, 8, 128), F32),
            dma((7,)),
            dma((ROWS_Y, 2)),
            dma((ROWS_Y, 2)),
            dma((2, 2, 2, 4)),
            dma((2, 2, 2, 4)),
            dma((ROWS_Y, 2)),
            dma((ROWS_Y, 2)),
            dma((ROWS_Y, 2)),
            dma((ROWS_Y, 2)),
            dma((2,)),
            dma((2,)),
            dma((2,)),
            dma((2,)),
            dma((2, GROUP)),
            dma((2, GROUP)),
        ],
        compiler_params=pltpu.CompilerParams(
            collective_id=0, has_side_effects=True, vmem_limit_bytes=56 * 2**20
        ),
    )(
        q.reshape(2, SPAN, WIDE),
        k.reshape(2, SPAN, HD),
        v.reshape(2, SPAN, HD),
        lq.reshape(2, SPAN, WIDE),
        lk.reshape(2, SPAN, WIDE),
        shrink,
        fading,
        gain.reshape(1, WIDE),
    )
    return out.reshape(2 * SPAN, WIDE)


def solution(mesh):
    placed = (
        P("ctx", "head"),
        P("ctx", "head"),
        P("ctx", "head"),
        P("ctx", "head"),
        P("ctx", "head"),
        P("head"),
        P("ctx"),
        P("head"),
    )
    return jax.shard_map(
        per_device, mesh=mesh, in_specs=placed, out_specs=P("ctx", "head"), check_vma=False
    )
```
